32 devices in a mesh: grp: 2 (over core), row: 4 (over y, x), col: 4 (over z).
Axes of the slice: x: 2, y: 2, z: 4, core: 2. Of those that a mesh axis runs over, the one named last changes fastest.
Arguments:
- iterate: bfloat16 [8192, 7168], P(('grp', 'row'), 'col'), parts along dimension 0, may hold values from -0.046875 to 0.046875
Outputs:
- update: bfloat16 [8192, 7168], P(('grp', 'row'), 'col'), parts along dimension 0
The draws below stay inside these ranges and needn't reach their ends.
There are 2 independent parts, one for each index of `grp`. The reference program is written for one: setup_inputs(seed, part) draws one part's arguments, and reference() takes and returns one part's arrays. A program takes and returns all parts, laid end to end along the dimension named above; each array names one. Nothing has to cross between parts.
All inputs are finite; a program needn't handle non-finite values.
Results may differ from the reference program's by a relative error of at most 0.0076.
Values may be sent and summed in bfloat16 or wider, within the bound.
A program may use at most 128 MiB of HBM per device.

```python
import math
import jax
import jax.numpy as jnp

HEAD_FEATS = 4096
MODEL_DIM = 7168


def shard_levels(stream_key, extent, cuts, least, high):
    gain = 1.0
    for axis_at, parts in cuts:
        draws = jax.random.uniform(jax.random.fold_in(jax.random.fold_in(stream_key, 6), axis_at), (parts,), jnp.float32, least / len(cuts), high / len(cuts))
        gain = gain * jnp.repeat(jnp.exp(draws), extent[axis_at] // parts).reshape((-1,) + (1,) * (len(extent) - 1 - axis_at))
    return gain


def normal_values(stream_key, shape, spread, bound, shards=(), dtype=jnp.bfloat16):
    array = spread * jax.random.normal(stream_key, shape, jnp.float32)
    if shards:
        array = array * shard_levels(stream_key, shape, shards, -0.22, 0.18)
    return jnp.clip(array, -bound, bound).astype(dtype)


def setup_inputs(seed: int = 0, part: int = 0) -> dict:
    keys = jax.random.split(jax.random.key(seed), 2)
    part_keys = jax.random.split(jax.random.fold_in(keys[1], part), 2)
    iterate = normal_values(part_keys[0], (HEAD_FEATS, MODEL_DIM), (2 * MODEL_DIM) ** -0.5, 0.046875, ((0, 4), (1, 4)))
    return {"iterate": iterate}


quintic_first = 3.4445
quintic_third = -4.775
quintic_fifth = 2.0315

def reference(iterate):
    gram = jnp.dot(iterate, iterate.T, preferred_element_type=jnp.float32)
    gram_half = gram.astype(jnp.bfloat16)
    square = jnp.dot(gram_half, gram_half, preferred_element_type=jnp.float32)
    poly = (quintic_third * gram + quintic_fifth * square).astype(jnp.bfloat16)
    mixed = jnp.dot(poly, iterate, preferred_element_type=jnp.float32)
    factor = 0.2 * math.sqrt(max(HEAD_FEATS, MODEL_DIM))
    update = factor * (quintic_first * iterate.astype(jnp.float32) + mixed)
    return update.astype(jnp.bfloat16)
```

```python
import math

import jax
import jax.numpy as jnp
from jax import lax
from jax.sharding import PartitionSpec as P

HEAD_FEATS = 4096
MODEL_DIM = 7168


quintic_first = 3.4445
quintic_third = -4.775
quintic_fifth = 2.0315

ROW_SETS = 2
PANELS = 2


def shards(iterate):
    rows, feats = iterate.shape
    sets = []
    for s in range(ROW_SETS):
        take = rows // ROW_SETS
        block = lax.all_gather(iterate[s * take : (s + 1) * take], "row", axis=0, tiled=True)
        partial = lax.dot_general(
            block, iterate, (((1,), (1,)), ((), ())), preferred_element_type=jnp.float32
        ).astype(jnp.bfloat16)
        owned = lax.psum_scatter(partial, "col", scatter_dimension=0, tiled=True)
        gram = lax.all_gather(owned, "col", axis=0, tiled=True)
        sets.append((block, gram))
    panel = jnp.concatenate([block for block, _ in sets], axis=0)
    gram_rows = jnp.concatenate([gram for _, gram in sets], axis=0).T
    factor = 0.2 * math.sqrt(max(HEAD_FEATS, MODEL_DIM))
    take = rows // ROW_SETS
    updates = []
    for p in range(PANELS):
        width = feats // PANELS
        columns = slice(p * width, (p + 1) * width)
        own = iterate[:, columns].astype(jnp.float32)
        once = jnp.dot(gram_rows, panel[:, columns], preferred_element_type=jnp.float32)
        inner = (quintic_third * own + quintic_fifth * once).astype(jnp.bfloat16)
        gathered = jnp.concatenate(
            [
                lax.all_gather(inner[s * take : (s + 1) * take], "row", axis=0, tiled=True)
                for s in range(ROW_SETS)
            ],
            axis=0,
        )
        mixed = jnp.dot(gram_rows, gathered, preferred_element_type=jnp.float32)
        updates.append((factor * (quintic_first * own + mixed)).astype(jnp.bfloat16))
    return jnp.concatenate(updates, axis=1)


def solution(mesh):
    in_specs = (P(("grp", "row"), "col"),)
    out_specs = P(("grp", "row"), "col")
    return jax.shard_map(shards, mesh=mesh, in_specs=in_specs, out_specs=out_specs, check_vma=False)
```

```python
import math

import jax
import jax.numpy as jnp
from jax import lax
from jax.sharding import PartitionSpec as P

HEAD_FEATS = 4096
MODEL_DIM = 7168


quintic_first = 3.4445
quintic_third = -4.775
quintic_fifth = 2.0315


def swap(block, offset, count):
    return lax.ppermute(block, "row", [(i, i ^ offset) for i in range(count)])


def gather_blocks(block, count):
    half = block.shape[0] // 2
    blocks = [block]
    for offset in range(1, count):
        top = 1 << (offset.bit_length() - 1)
        low = offset & -offset
        if top == offset:
            blocks.append(swap(block, offset, count))
        else:
            first = swap(blocks[offset ^ top][:half], top, count)
            second = swap(blocks[offset ^ low][half:], low, count)
            blocks.append(jnp.concatenate([first, second], axis=0))
    return blocks


def times_transpose(left, right):
    return lax.dot_general(
        left, right, (((1,), (1,)), ((), ())), preferred_element_type=jnp.float32
    )


def sum_over_columns(partial):
    owned = lax.psum_scatter(partial.astype(jnp.bfloat16), "col", scatter_dimension=0, tiled=True)
    return lax.all_gather(owned, "col", axis=0, tiled=True)


def shards(iterate):
    count = lax.axis_size("row")
    rows = iterate.shape[0]
    half = rows // 2
    me = lax.axis_index("row")
    wide = iterate.astype(jnp.float32)
    blocks = gather_blocks(iterate, count)

    diagonal = lax.psum(jnp.sum(wide * wide, axis=1, keepdims=True), "col")
    eye = lax.broadcasted_iota(jnp.int32, (rows, rows), 0) == lax.broadcasted_iota(
        jnp.int32, (rows, rows), 1
    )
    gram = [sum_over_columns(jnp.where(eye, 0.0, times_transpose(iterate, iterate)))]
    for offset in range(1, count):
        lower = (me & (1 << (offset.bit_length() - 1))) == 0
        other = blocks[offset]
        tall = jnp.where(lower, iterate, other)
        short = jnp.where(lower, other[:half], iterate[half:])
        mine = sum_over_columns(times_transpose(short, tall))
        theirs = swap(mine, offset, count)
        pair = jnp.concatenate(
            [jnp.where(lower, mine, theirs), jnp.where(lower, theirs, mine)], axis=0
        )
        gram.append(jnp.where(lower, pair.T, pair))

    def apply_gram(own, parts):
        total = diagonal * own
        for block, part in zip(gram, parts):
            total = total + jnp.dot(block, part, preferred_element_type=jnp.float32)
        return total

    inner = quintic_third * wide + quintic_fifth * apply_gram(wide, blocks)
    mixed = apply_gram(inner, gather_blocks(inner.astype(jnp.bfloat16), count))
    factor = 0.2 * math.sqrt(max(HEAD_FEATS, MODEL_DIM))
    return (factor * (quintic_first * wide + mixed)).astype(jnp.bfloat16)


def solution(mesh):
    in_specs = (P(("grp", "row"), "col"),)
    out_specs = P(("grp", "row"), "col")
    return jax.shard_map(shards, mesh=mesh, in_specs=in_specs, out_specs=out_specs, check_vma=False)
```

```python
import math

import jax
import jax.numpy as jnp
from jax import lax
from jax.sharding import PartitionSpec as P

HEAD_FEATS = 4096
MODEL_DIM = 7168


quintic_first = 3.4445
quintic_third = -4.775
quintic_fifth = 2.0315

PANELS = 2


def swap(block, offset, count):
    return lax.ppermute(block, "row", [(i, i ^ offset) for i in range(count)])


def gather_blocks(block, count):
    half = block.shape[0] // 2
    blocks = [block]
    for offset in range(1, count):
        top = 1 << (offset.bit_length() - 1)
        low = offset & -offset
        if top == offset:
            blocks.append(swap(block, offset, count))
        else:
            first = swap(blocks[offset ^ top][:half], top, count)
            second = swap(blocks[offset ^ low][half:], low, count)
            blocks.append(jnp.concatenate([first, second], axis=0))
    return blocks


def times_transpose(left, right):
    return lax.dot_general(
        left, right, (((1,), (1,)), ((), ())), preferred_element_type=jnp.float32
    )


def sum_over_columns(partial):
    owned = lax.psum_scatter(partial.astype(jnp.bfloat16), "col", scatter_dimension=0, tiled=True)
    return lax.all_gather(owned, "col", axis=0, tiled=True)


def shards(iterate):
    count = lax.axis_size("row")
    rows = iterate.shape[0]
    half = rows // 2
    me = lax.axis_index("row")
    wide = iterate.astype(jnp.float32)
    blocks = gather_blocks(iterate, count)

    diagonal = lax.psum(jnp.sum(wide * wide, axis=1, keepdims=True), "col")
    eye = lax.broadcasted_iota(jnp.int32, (rows, rows), 0) == lax.broadcasted_iota(
        jnp.int32, (rows, rows), 1
    )
    own = jnp.where(eye, 0.0, times_transpose(iterate, iterate))
    packed = sum_over_columns(jnp.concatenate([own[half:], own[:half, :half]], axis=1))
    gram = [
        jnp.concatenate(
            [
                jnp.concatenate([packed[:, rows:], packed[:, :half].T], axis=1),
                packed[:, :rows],
            ],
            axis=0,
        )
    ]
    arrived = [lax.optimization_barrier((packed, block))[1] for block in blocks[1:]]
    for offset in range(1, count):
        lower = (me & (1 << (offset.bit_length() - 1))) == 0
        other = arrived[offset - 1]
        tall = jnp.where(lower, iterate, other)
        short = jnp.where(lower, other[:half], iterate[half:])
        mine = sum_over_columns(times_transpose(short, tall))
        theirs = swap(mine, offset, count)
        pair = jnp.concatenate(
            [jnp.where(lower, mine, theirs), jnp.where(lower, theirs, mine)], axis=0
        )
        gram.append(jnp.where(lower, pair.T, pair))

    def apply_gram(own, parts):
        total = diagonal * own
        for block, part in zip(gram, parts):
            total = total + jnp.dot(block, part, preferred_element_type=jnp.float32)
        return total

    factor = 0.2 * math.sqrt(max(HEAD_FEATS, MODEL_DIM))
    width = iterate.shape[1] // PANELS
    updates = []
    for p in range(PANELS):
        columns = slice(p * width, (p + 1) * width)
        own = wide[:, columns]
        once = apply_gram(own, [block[:, columns] for block in blocks])
        inner = quintic_third * own + quintic_fifth * once
        mixed = apply_gram(inner, gather_blocks(inner.astype(jnp.bfloat16), count))
        updates.append((factor * (quintic_first * own + mixed)).astype(jnp.bfloat16))
    return jnp.concatenate(updates, axis=1)


def solution(mesh):
    in_specs = (P(("grp", "row"), "col"),)
    out_specs = P(("grp", "row"), "col")
    return jax.shard_map(shards, mesh=mesh, in_specs=in_specs, out_specs=out_specs, check_vma=False)
```

```python
import math

import jax
import jax.numpy as jnp
from jax import lax
from jax.sharding import PartitionSpec as P

HEAD_FEATS = 4096
MODEL_DIM = 7168


quintic_first = 3.4445
quintic_third = -4.775
quintic_fifth = 2.0315

PANELS = 2


def swap(block, offset, count):
    return lax.ppermute(block, "row", [(i, i ^ offset) for i in range(count)])


def gather_blocks(block, count):
    half = block.shape[0] // 2
    blocks = [block]
    for offset in range(1, count):
        top = 1 << (offset.bit_length() - 1)
        low = offset & -offset
        if top == offset:
            blocks.append(swap(block, offset, count))
        else:
            first = swap(blocks[offset ^ top][:half], top, count)
            second = swap(blocks[offset ^ low][half:], low, count)
            blocks.append(jnp.concatenate([first, second], axis=0))
    return blocks


def times_transpose(left, right):
    return lax.dot_general(
        left, right, (((1,), (1,)), ((), ())), preferred_element_type=jnp.float32
    )


def sum_over_columns(partial):
    owned = lax.psum_scatter(partial.astype(jnp.bfloat16), "col", scatter_dimension=0, tiled=True)
    return lax.all_gather(owned, "col", axis=0, tiled=True)


def shards(iterate):
    count = lax.axis_size("row")
    rows = iterate.shape[0]
    half = rows // 2
    me = lax.axis_index("row")
    wide = iterate.astype(jnp.float32)
    blocks = gather_blocks(iterate, count)

    diagonal = lax.psum(jnp.sum(wide * wide, axis=1, keepdims=True), "col")
    eye = lax.broadcasted_iota(jnp.int32, (rows, rows), 0) == lax.broadcasted_iota(
        jnp.int32, (rows, rows), 1
    )
    own = jnp.where(eye, 0.0, times_transpose(iterate, iterate))
    packed = sum_over_columns(jnp.concatenate([own[half:], own[:half, :half]], axis=1))
    gram = [
        jnp.concatenate(
            [
                jnp.concatenate([packed[:, rows:], packed[:, :half].T], axis=1),
                packed[:, :rows],
            ],
            axis=0,
        )
    ]
    before = packed
    for offset in range(1, count):
        lower = (me & (1 << (offset.bit_length() - 1))) == 0
        before, other = lax.optimization_barrier((before, blocks[offset]))
        tall = jnp.where(lower, iterate, other)
        short = jnp.where(lower, other[:half], iterate[half:])
        before = times_transpose(short, tall).astype(jnp.bfloat16)
        mine = sum_over_columns(before)
        theirs = swap(mine, offset, count)
        pair = jnp.concatenate(
            [jnp.where(lower, mine, theirs), jnp.where(lower, theirs, mine)], axis=0
        )
        gram.append(jnp.where(lower, pair.T, pair))

    def apply_gram(own, parts):
        total = diagonal * own
        for block, part in zip(gram, parts):
            total = total + jnp.dot(block, part, preferred_element_type=jnp.float32)
        return total

    factor = 0.2 * math.sqrt(max(HEAD_FEATS, MODEL_DIM))
    width = iterate.shape[1] // PANELS
    updates = []
    for p in range(PANELS):
        columns = slice(p * width, (p + 1) * width)
        own = wide[:, columns]
        once = apply_gram(own, [block[:, columns] for block in blocks])
        inner = quintic_third * own + quintic_fifth * once
        mixed = apply_gram(inner, gather_blocks(inner.astype(jnp.bfloat16), count))
        updates.append((factor * (quintic_first * own + mixed)).astype(jnp.bfloat16))
    return jnp.concatenate(updates, axis=1)


def solution(mesh):
    in_specs = (P(("grp", "row"), "col"),)
    out_specs = P(("grp", "row"), "col")
    return jax.shard_map(shards, mesh=mesh, in_specs=in_specs, out_specs=out_specs, check_vma=False)
```

```python
import math

import jax
import jax.numpy as jnp
from jax import lax
from jax.sharding import PartitionSpec as P

HEAD_FEATS = 4096
MODEL_DIM = 7168


quintic_first = 3.4445
quintic_third = -4.775
quintic_fifth = 2.0315

PANELS = 2


def swap(block, offset, count):
    return lax.ppermute(block, "row", [(i, i ^ offset) for i in range(count)])


def gather_blocks(block, count):
    half = block.shape[0] // 2
    blocks = [block]
    for offset in range(1, count):
        top = 1 << (offset.bit_length() - 1)
        low = offset & -offset
        if top == offset:
            blocks.append(swap(block, offset, count))
        else:
            first = swap(blocks[offset ^ top][:half], top, count)
            second = swap(blocks[offset ^ low][half:], low, count)
            blocks.append(jnp.concatenate([first, second], axis=0))
    return blocks


def times_transpose(left, right):
    return lax.dot_general(
        left, right, (((1,), (1,)), ((), ())), preferred_element_type=jnp.float32
    )


def sum_over_columns(partial):
    owned = lax.psum_scatter(partial.astype(jnp.bfloat16), "col", scatter_dimension=0, tiled=True)
    return lax.all_gather(owned, "col", axis=0, tiled=True)


def shards(iterate):
    count = lax.axis_size("row")
    rows = iterate.shape[0]
    half = rows // 2
    me = lax.axis_index("row")
    wide = iterate.astype(jnp.float32)
    blocks = gather_blocks(iterate, count)

    diagonal = lax.psum(jnp.sum(wide * wide, axis=1, keepdims=True), "col")
    eye = lax.broadcasted_iota(jnp.int32, (rows, rows), 0) == lax.broadcasted_iota(
        jnp.int32, (rows, rows), 1
    )
    own = jnp.where(eye, 0.0, times_transpose(iterate, iterate))
    packed = sum_over_columns(jnp.concatenate([own[half:], own[:half, :half]], axis=1))
    gram = [
        jnp.concatenate(
            [
                jnp.concatenate([packed[:, rows:], packed[:, :half].T], axis=1),
                packed[:, :rows],
            ],
            axis=0,
        )
    ]
    direct = [offset for offset in range(1, count) if offset & (offset - 1) == 0]
    distant = [offset for offset in range(1, count) if offset & (offset - 1) != 0]
    found = {}
    before = packed
    for offsets in (direct, distant):
        partials = []
        for offset in offsets:
            lower = (me & (1 << (offset.bit_length() - 1))) == 0
            other = lax.optimization_barrier((before, blocks[offset]))[1]
            tall = jnp.where(lower, iterate, other)
            short = jnp.where(lower, other[:half], iterate[half:])
            partials.append(times_transpose(short, tall).astype(jnp.bfloat16))
        if not partials:
            continue
        before = lax.psum_scatter(
            jnp.concatenate(partials, axis=1), "col", scatter_dimension=0, tiled=True
        )
        summed = lax.all_gather(before, "col", axis=0, tiled=True)
        for at, offset in enumerate(offsets):
            lower = (me & (1 << (offset.bit_length() - 1))) == 0
            mine = summed[:, at * rows : (at + 1) * rows]
            theirs = swap(mine, offset, count)
            pair = jnp.concatenate(
                [jnp.where(lower, mine, theirs), jnp.where(lower, theirs, mine)], axis=0
            )
            found[offset] = jnp.where(lower, pair.T, pair)
    gram += [found[offset] for offset in range(1, count)]

    def apply_gram(own, parts):
        total = diagonal * own
        for block, part in zip(gram, parts):
            total = total + jnp.dot(block, part, preferred_element_type=jnp.float32)
        return total

    factor = 0.2 * math.sqrt(max(HEAD_FEATS, MODEL_DIM))
    width = iterate.shape[1] // PANELS
    updates = []
    for p in range(PANELS):
        columns = slice(p * width, (p + 1) * width)
        own = wide[:, columns]
        once = apply_gram(own, [block[:, columns] for block in blocks])
        inner = quintic_third * own + quintic_fifth * once
        mixed = apply_gram(inner, gather_blocks(inner.astype(jnp.bfloat16), count))
        updates.append((factor * (quintic_first * own + mixed)).astype(jnp.bfloat16))
    return jnp.concatenate(updates, axis=1)


def solution(mesh):
    in_specs = (P(("grp", "row"), "col"),)
    out_specs = P(("grp", "row"), "col")
    return jax.shard_map(shards, mesh=mesh, in_specs=in_specs, out_specs=out_specs, check_vma=False)
```
